128 devices in a mesh: ctx: 8 (over y, core), head: 16 (over x, z).
Axes of the slice: x: 4, y: 4, z: 4, core: 2. Of those that a mesh axis runs over, the one named last changes fastest.
Arguments:
- ssm_input: bfloat16 [16384, 16384], P('ctx', 'head'), may hold values from -6 to 6
- step_size: float32 [16384, 256], P('ctx', 'head'), may hold values from 0.0625 to 16
- decay_rate: float32 [256], P('head'), may hold values from 2e-05 to 0.04
- skip_gain: float32 [256], P('head'), may hold values from 0.5 to 1.5
- input_proj: bfloat16 [16384, 8, 256], P('ctx'), may hold values from -0.375 to 0.375
- output_proj: bfloat16 [16384, 8, 256], P('ctx'), may hold values from -0.375 to 0.375
- out_grad: bfloat16 [16384, 16384], P(('ctx', 'head')), may hold values from -3 to 3
Outputs:
- input_grad: bfloat16 [16384, 16384], P(('ctx', 'head'))
- step_grad: float32 [16384, 256], P('ctx', 'head')
The draws below stay inside these ranges and needn't reach their ends.
All inputs are finite; a program needn't handle non-finite values.
Results may differ from the reference program's by a relative error of at most 0.001.
Values may be sent and summed in bfloat16 or wider, within the bound.
A program may use at most 256 MiB of HBM per device.

```python
import math
import jax
import jax.numpy as jnp
from jax import lax

H = 256
P_SIZE = 64
N = 256
G = 8
SPAN = 256
LDEV = 2048
L = 16384


def draw_step_size(key, part):
    key = jax.random.fold_in(key, 11)
    base_key, block_key = jax.random.split(key)
    nblocks = L // LDEV
    base = jnp.exp(jax.random.uniform(base_key, (L, H), jnp.float32, jnp.log(0.5), jnp.log(2.0)))
    factor = jnp.exp(jax.random.uniform(block_key, (nblocks, 1, H), jnp.float32, jnp.log(0.25), jnp.log(4.0)))
    return (base.reshape(nblocks, LDEV, H) * factor).reshape(L, H)


def steps_of(key, dims, pieces, low, largest):
    def one(dim, shards_of):
        heights = jax.random.uniform(jax.random.fold_in(jax.random.fold_in(key, 6), dim), (shards_of,), jnp.float32, low / len(pieces), largest / len(pieces))
        return jnp.repeat(jnp.exp(heights), dims[dim] // shards_of).reshape((-1,) + (1,) * (len(dims) - dim - 1))

    factor_of = one(*pieces[0])
    for cut in pieces[1:]:
        factor_of = factor_of * one(*cut)
    return factor_of


def noise(stream_key, dims, spread, most, pieces=(), held_as=jnp.bfloat16):
    entries = spread * jax.random.normal(stream_key, dims, jnp.float32)
    if pieces:
        entries = entries * steps_of(stream_key, dims, pieces, -0.22, 0.18)
    return jnp.clip(entries, -most, most).astype(held_as)


def setup_inputs(seed: int = 0) -> dict:
    keys = jax.random.split(jax.random.key(seed), 8)
    return {
        "ssm_input": noise(keys[0], (L, H * P_SIZE), 1.0, 6.0, ((0, 8), (1, 16))),
        "step_size": draw_step_size(jax.random.fold_in(keys[7], 71), 0),
        "decay_rate": jnp.clip(jnp.exp(math.log(0.04) - 7.6009025 * jax.random.uniform(keys[2], (H,), jnp.float32) ** steps_of(keys[2], (H,), ((0, 16),), -0.2, 0.2)), 1.9999999494757503e-05, 0.04),
        "skip_gain": jnp.clip(0.5 + 1.0 * jax.random.uniform(keys[3], (H,), jnp.float32) ** steps_of(keys[3], (H,), ((0, 16),), -0.2, 0.2), 0.5, 1.5),
        "input_proj": noise(keys[4], (L, G, N), N ** -0.5, 0.375, ((0, 8),)),
        "output_proj": noise(keys[5], (L, G, N), N ** -0.5, 0.375, ((0, 8),)),
        "out_grad": noise(keys[6], (L, H * P_SIZE), 0.5, 3.0, ((0, 128),)),
    }


def head_grads(head_id, ssm_input, step_size, decay_rate, skip_gain, input_proj, output_proj, out_grad):
    highest = lax.Precision.HIGHEST
    total_len = ssm_input.shape[0]
    nblocks = total_len // SPAN
    group_id = head_id // (H // G)
    head_in = lax.dynamic_slice_in_dim(ssm_input, head_id * P_SIZE, P_SIZE, 1).astype(jnp.float32).reshape(nblocks, SPAN, P_SIZE)
    head_grad = lax.dynamic_slice_in_dim(out_grad, head_id * P_SIZE, P_SIZE, 1).astype(jnp.float32).reshape(nblocks, SPAN, P_SIZE)
    head_step = lax.dynamic_slice_in_dim(step_size, head_id, 1, 1)[:, 0].reshape(nblocks, SPAN)
    proj_b = lax.dynamic_index_in_dim(input_proj, group_id, 1, keepdims=False).astype(jnp.float32).reshape(nblocks, SPAN, N)
    proj_c = lax.dynamic_index_in_dim(output_proj, group_id, 1, keepdims=False).astype(jnp.float32).reshape(nblocks, SPAN, N)
    head_rate = decay_rate[head_id]
    head_gain = skip_gain[head_id]
    cumulative = jnp.cumsum(-head_rate * head_step, axis=1)
    block_total = cumulative[:, -1]
    positions = jnp.arange(SPAN)
    lower_mask = positions[:, None] >= positions[None, :]
    log_ratio = cumulative[:, :, None] - cumulative[:, None, :]
    weights = jnp.exp(jnp.where(lower_mask[None], log_ratio, -jnp.inf))
    inner_prod = jnp.einsum('cqn,ckn->cqk', proj_c, proj_b, precision=highest) * weights
    fwd_term = jnp.einsum('cqp,cqn->cpn', head_in * (head_step * jnp.exp(block_total[:, None] - cumulative))[..., None], proj_b, precision=highest)
    back_term = jnp.einsum('cqp,cqn->cpn', head_grad * jnp.exp(cumulative)[..., None], proj_c, precision=highest)

    def chain_step(carried, element):
        return jnp.exp(element[0]) * carried + element[1], carried

    zero_state = jnp.zeros((P_SIZE, N), jnp.float32)
    _, starts = lax.scan(chain_step, zero_state, (block_total, fwd_term))
    _, block_ends = lax.scan(chain_step, zero_state, (block_total, back_term), reverse=True)
    scaled_in = head_in * head_step[..., None]
    out_value = jnp.einsum('cqk,ckp->cqp', inner_prod, scaled_in, precision=highest)
    out_value = out_value + jnp.exp(cumulative)[..., None] * jnp.einsum('cqn,cpn->cqp', proj_c, starts, precision=highest)
    adjoint = jnp.einsum('cqk,cqp->ckp', inner_prod, head_grad, precision=highest)
    adjoint = adjoint + jnp.exp(block_total[:, None] - cumulative)[..., None] * jnp.einsum('cqn,cpn->cqp', proj_b, block_ends, precision=highest)
    grad_head = (head_step[..., None] * adjoint + head_gain * head_grad).astype(jnp.bfloat16).reshape(total_len, P_SIZE)
    in_dot_adj = jnp.sum(head_in * adjoint, axis=-1).reshape(total_len)
    decay_grad = jnp.sum(head_grad * out_value, axis=-1).reshape(total_len) - head_step.reshape(total_len) * in_dot_adj
    tail_sums = jnp.flip(jnp.cumsum(jnp.flip(decay_grad)))
    return grad_head, in_dot_adj - head_rate * tail_sums


def reference(ssm_input, step_size, decay_rate, skip_gain, input_proj, output_proj, out_grad):
    total_len = ssm_input.shape[0]

    def per_head(head_id):
        return head_grads(head_id, ssm_input, step_size, decay_rate, skip_gain, input_proj, output_proj, out_grad)

    grads_heads, steps_heads = lax.map(per_head, jnp.arange(H, dtype=jnp.int32))
    input_grad = jnp.transpose(grads_heads, (1, 0, 2)).reshape(total_len, H * P_SIZE)
    return input_grad, jnp.transpose(steps_heads)
```

```python
import jax
import jax.numpy as jnp
from jax import lax
from jax.experimental import pallas as pl
from jax.experimental.pallas import tpu as pltpu
from jax.sharding import PartitionSpec as P

NHEAD = 16
NY = 4
LOCAL = 2048
ROWS = 128
COLS = 1024
BLK = 256
NBLK = LOCAL // BLK
GC = 256
NG = COLS // GC
NGROUPS = 8
CH = 128
NCH = LOCAL // CH
MESH = pl.DeviceIdType.MESH
F32 = jnp.float32
BF16 = jnp.bfloat16


def mm(a, b):
    return jnp.dot(a, b, preferred_element_type=F32)


def exact_mm(a, b):
    return jnp.dot(a, b, preferred_element_type=F32, precision=lax.Precision.HIGHEST)


def halves(v):
    hi = v.astype(BF16)
    return hi, (v - hi.astype(F32)).astype(BF16)


def iota(shape, dim):
    return lax.broadcasted_iota(jnp.int32, shape, dim)


def pack3(v):
    hi = v.astype(BF16).astype(F32)
    rest = v - hi
    md = rest.astype(BF16).astype(F32)
    parts = jnp.concatenate([hi, md, rest - md, jnp.zeros((80, v.shape[1]), F32)], axis=0)
    return parts.T.astype(BF16)


def kernel(
    x_hbm, step_ref, rate_ref, gain_ref, b_hbm, c_hbm, g_hbm, out_hbm, sg_ref,
    xo, gv, xh, xl, agh, agl, tf, ta, raw, bm, cm, bt, ct, cbh, cbl, bch, bcl,
    asp, bsp, expand, acc, res, qe, we, de, lbuf,
    fs_tot, fs_pair, fs_chip, fs_in, as_tot, as_pair, as_chip, as_in,
    loc_sem, raw_sem, gs, gr, os, orr, ls, lr, fps, fpr, fys, fyr, aps, apr, ays, ayr,
):
    c = lax.axis_index("ctx")
    h = lax.axis_index("head")
    hx, hz = h // 4, lax.rem(h, 4)
    y, k = c // 2, lax.rem(c, 2)
    group = h // 2
    core0 = k == 0

    def head_at(j):
        return lax.rem(hx + j // 4, 4) * 4 + lax.rem(hz + lax.rem(j, 4), 4)

    def head_from(j):
        return lax.rem(hx + 4 - j // 4, 4) * 4 + lax.rem(hz + 4 - lax.rem(j, 4), 4)

    def cols(grp):
        return pl.ds(grp * GC, GC)

    x_copy = pltpu.make_async_copy(x_hbm, xo, loc_sem.at[0])
    x_copy.start()

    def raw_copies(i):
        rows = pl.ds(pl.multiple_of(i * (CH * NGROUPS), CH * NGROUPS), CH * NGROUPS)
        slot = lax.rem(i, 2)
        return (
            pltpu.make_async_copy(b_hbm.at[rows], raw.at[slot, 0], raw_sem.at[slot, 0]),
            pltpu.make_async_copy(c_hbm.at[rows], raw.at[slot, 1], raw_sem.at[slot, 1]),
        )

    for cp in raw_copies(0):
        cp.start()

    barrier = pltpu.get_barrier_semaphore()

    @pl.loop(1, NHEAD)
    def _(j):
        pl.semaphore_signal(barrier, 1, device_id=(c, head_at(j)), device_id_type=MESH)

    @pl.loop(1, 8)
    def _(j):
        pl.semaphore_signal(barrier, 1, device_id=(lax.rem(c + j, 8), h), device_id_type=MESH)

    pl.semaphore_wait(barrier, NHEAD - 1 + 7)

    def grad_in(grp, j):
        to = head_at(j)
        return pltpu.make_async_remote_copy(
            g_hbm.at[:, pl.ds(pl.multiple_of(to * COLS + grp * GC, GC), GC)],
            gv.at[pl.ds(pl.multiple_of(h * ROWS, ROWS), ROWS), cols(grp)],
            gs.at[grp, j],
            gr.at[grp, j],
            device_id=(c, to),
            device_id_type=MESH,
        )

    for grp in range(NG):

        @pl.loop(1, NHEAD)
        def _(j):
            grad_in(grp, j).start()

    own_g = pltpu.make_async_copy(
        g_hbm.at[:, pl.ds(pl.multiple_of(h * COLS, COLS), COLS)],
        gv.at[pl.ds(pl.multiple_of(h * ROWS, ROWS), ROWS)],
        loc_sem.at[1],
    )
    own_g.start()

    eye16 = iota((16, 16), 0) == iota((16, 16), 1)
    rate = jnp.sum(jnp.where(eye16, rate_ref[...], 0.0), axis=1, keepdims=True)
    gain = jnp.sum(jnp.where(eye16, gain_ref[...], 0.0), axis=1, keepdims=True)
    kk = iota((128, COLS), 0)
    expand[...] = jnp.where(
        (kk < 48) & (lax.rem(kk, 16) == iota((128, COLS), 1) // 64), 1.0, 0.0
    ).astype(BF16)
    before = (iota((BLK, BLK), 0) <= iota((BLK, BLK), 1)).astype(F32)
    lane = iota((16, 128), 1)
    mids = jnp.zeros((16, 128), F32)
    log_own = jnp.zeros((16, 1), F32)
    for blk in range(NBLK):
        st = step_ref[:, blk * BLK : (blk + 1) * BLK]
        cum = exact_mm(-rate * st, before)
        total = cum[:, BLK - 1 : BLK]
        mid = 0.5 * total
        mids = jnp.where(lane == blk, mid, mids)
        log_own = log_own + total
        asp[blk] = pack3(jnp.exp(cum - mid))
        bsp[blk] = pack3(st * jnp.exp(mid - cum) * 0.0625)
    qe[...] = mm(pack3(jnp.where(lane == 8, gain, jnp.exp(mids)))[:16], expand[...])
    lbuf[c] = jnp.broadcast_to(log_own, (16, 128))

    def log_send(j):
        return pltpu.make_async_remote_copy(
            lbuf.at[c], lbuf.at[c], ls.at[j], lr.at[j],
            device_id=(lax.rem(c + j, 8), h), device_id_type=MESH,
        )

    @pl.loop(1, 8)
    def _(j):
        log_send(j).start()

    pick = jnp.where(iota((32, 256), 1) == iota((32, 256), 0) * NGROUPS + group, 1.0, 0.0)
    pick = pick.astype(BF16)

    @pl.loop(0, NCH)
    def _(i):
        @pl.when(i + 1 < NCH)
        def _():
            for cp in raw_copies(i + 1):
                cp.start()

        for cp in raw_copies(i):
            cp.wait()
        slot = lax.rem(i, 2)
        at = pl.multiple_of(i * CH, CH)
        for which, target in ((0, bm), (1, cm)):
            for part in range(CH // 32):
                rows = raw[slot, which, pl.ds(part * 256, 256), :]
                target[pl.ds(at + part * 32, 32), :] = mm(pick, rows).astype(BF16)

    low = iota((BLK, BLK), 0) >= iota((BLK, BLK), 1)

    @pl.loop(0, NBLK)
    def _(blk):
        at = pl.ds(pl.multiple_of(blk * BLK, BLK), BLK)
        b, cc = bm[at, :], cm[at, :]
        btr, ctr = b.T, cc.T
        bt[at, :] = btr
        ct[at, :] = ctr
        cbh[at, :], cbl[at, :] = halves(jnp.where(low, mm(cc, btr), 0.0))
        bch[at, :], bcl[at, :] = halves(jnp.where(low, mm(cc, btr), 0.0).T)

    def pair_copy(src, dst, s, r, grp):
        return pltpu.make_async_remote_copy(
            src.at[grp], dst.at[grp], s.at[grp], r.at[grp],
            device_id=(y * 2 + 1 - k, h), device_id_type=MESH,
        )

    def line_copy(src, dst, s, r, grp, dy, forward):
        to = y + dy if forward else y + 4 - dy
        return pltpu.make_async_remote_copy(
            src.at[grp], dst.at[dy - 1, grp], s.at[dy - 1, grp], r.at[dy - 1, grp],
            device_id=(lax.rem(to, 4) * 2 + k, h), device_id_type=MESH,
        )

    def q_row(blk, grp):
        return qe[pl.ds(blk, 1), cols(grp)]

    def forward_local(grp):
        acc[...] = jnp.zeros_like(acc)

        @pl.loop(0, NBLK)
        def _(blk):
            at = pl.ds(pl.multiple_of(blk * BLK, BLK), BLK)
            xb = xo[at, cols(grp)].astype(F32) * mm(bsp[blk], expand[:, cols(grp)])
            hi, lo = halves(xb)
            xh[at, cols(grp)] = hi
            xl[at, cols(grp)] = lo
            t = mm(bt[at, :], hi) + mm(bt[at, :], lo)
            tf[grp, blk] = t
            q = q_row(blk, grp)
            acc[...] = q * (q * acc[...] + t)

        fs_tot[grp] = acc[...]
        pair_copy(fs_tot, fs_pair, fps, fpr, grp).start()

    def forward_chip(grp):
        pair_copy(fs_tot, fs_pair, fps, fpr, grp).wait()
        fs_chip[grp] = (
            we[0:1, cols(grp)] * fs_tot[grp] + we[1:2, cols(grp)] * fs_pair[grp]
        ).astype(BF16)
        for dy in (1, 2, 3):

            @pl.when(y + dy < NY)
            def _():
                line_copy(fs_chip, fs_in, fys, fyr, grp, dy, True).start()

    def forward_states(grp):
        acc[...] = jnp.zeros_like(acc)
        for dy in (1, 2, 3):

            @pl.when(y - dy >= 0)
            def _():
                line_copy(fs_chip, fs_in, fys, fyr, grp, dy, True).wait_recv()
                acc[...] += we[2 + dy : 3 + dy, cols(grp)] * fs_in[dy - 1, grp].astype(F32)

        acc[...] = we[2:3, cols(grp)] * acc[...]

        @pl.when(k == 1)
        def _():
            acc[...] += fs_pair[grp]

        @pl.loop(0, NBLK)
        def _(blk):
            q = q_row(blk, grp)
            scaled = q * acc[...]
            acc[...] = q * (scaled + tf[grp, blk])
            tf[grp, blk] = scaled

        fs_tot[grp] = acc[...]

    def adjoint_local(grp):
        slot = grp % 2

        @pl.loop(1, NHEAD)
        def _(j):
            grad_in(grp, j).wait_recv()

        acc[...] = jnp.zeros_like(acc)

        @pl.loop(0, NBLK)
        def _(i):
            blk = NBLK - 1 - i
            at = pl.ds(pl.multiple_of(blk * BLK, BLK), BLK)
            ag = gv[at, cols(grp)].astype(F32) * mm(asp[blk], expand[:, cols(grp)])
            hi, lo = halves(ag)
            agh[slot, at, :] = hi
            agl[slot, at, :] = lo
            t = mm(ct[at, :], hi) + mm(ct[at, :], lo)
            ta[slot, blk] = t
            q = q_row(blk, grp)
            acc[...] = q * (q * acc[...] + t)

        as_tot[grp] = acc[...]
        pair_copy(as_tot, as_pair, aps, apr, grp).start()

    def adjoint_chip(grp):
        pair_copy(as_tot, as_pair, aps, apr, grp).wait()
        as_chip[grp] = we[6:7, cols(grp)] * as_tot[grp] + we[7:8, cols(grp)] * as_pair[grp]
        for dy in (1, 2, 3):

            @pl.when(y - dy >= 0)
            def _():
                line_copy(as_chip, as_in, ays, ayr, grp, dy, False).start()

    def grad_out(grp, j):
        to = head_at(j)
        return pltpu.make_async_remote_copy(
            xo.at[pl.ds(pl.multiple_of(to * ROWS, ROWS), ROWS), cols(grp)],
            out_hbm.at[:, pl.ds(pl.multiple_of(h * COLS + grp * GC, GC), GC)],
            os.at[grp, j],
            orr.at[grp, j],
            device_id=(c, to),
            device_id_type=MESH,
        )

    def own_out(grp):
        return pltpu.make_async_copy(
            xo.at[pl.ds(pl.multiple_of(h * ROWS, ROWS), ROWS), cols(grp)],
            out_hbm.at[:, pl.ds(pl.multiple_of(h * COLS + grp * GC, GC), GC)],
            loc_sem.at[2 + grp],
        )

    def finish(grp):
        slot = grp % 2
        acc[...] = jnp.zeros_like(acc)
        for dy in (1, 2, 3):

            @pl.when(y + dy < NY)
            def _():
                line_copy(as_chip, as_in, ays, ayr, grp, dy, False).wait_recv()
                acc[...] += we[8 + dy : 9 + dy, cols(grp)] * as_in[dy - 1, grp]

        acc[...] = we[8:9, cols(grp)] * acc[...]

        @pl.when(core0)
        def _():
            acc[...] += as_pair[grp]

        de[:, cols(grp)] = jnp.broadcast_to(
            jnp.sum(fs_tot[grp] * acc[...], axis=0, keepdims=True), (8, GC)
        )
        gain_row = qe[8:9, cols(grp)]
        head_of = grp * (GC // 64) + iota((GC, 128), 0) // 64
        to_dc = jnp.where(iota((GC, 128), 1) == head_of, 1.0, 0.0).astype(BF16)
        to_sx = jnp.where(iota((GC, 128), 1) == head_of + 64, 1.0, 0.0).astype(BF16)

        @pl.loop(0, NBLK)
        def _(i):
            blk = NBLK - 1 - i
            at = pl.ds(pl.multiple_of(blk * BLK, BLK), BLK)
            q = q_row(blk, grp)
            scaled = q * acc[...]
            acc[...] = q * (scaled + ta[slot, blk])
            sh, sl = halves(scaled)
            ah, al = agh[slot, at, :], agl[slot, at, :]
            b = bm[at, :]
            gb = mm(bch[at, :], ah) + mm(bcl[at, :], ah) + mm(bch[at, :], al)
            gb = gb + mm(b, sh) + mm(b, sl)
            bs = mm(bsp[blk], expand[:, cols(grp)])
            grads = (16.0 * bs) * gb + gain_row * gv[at, cols(grp)].astype(F32)
            xo[at, cols(grp)] = grads.astype(BF16)
            hi, lo = xh[at, cols(grp)], xl[at, cols(grp)]
            sh, sl = halves(tf[grp, blk])
            cc = cm[at, :]
            yy = mm(cbh[at, :], hi) + mm(cbl[at, :], hi) + mm(cbh[at, :], lo)
            yy = yy + mm(cc, sh) + mm(cc, sl)
            sx = (hi.astype(F32) + lo.astype(F32)) * gb
            dc = (ah.astype(F32) + al.astype(F32)) * yy - sx
            dh, dl = halves(dc)
            xh_, xl_ = halves(sx)
            r = mm(dh, to_dc) + mm(dl, to_dc) + mm(xh_, to_sx) + mm(xl_, to_sx)
            if grp == 0:
                res[blk] = r
            else:
                res[blk] += r

        @pl.loop(1, NHEAD)
        def _(j):
            grad_out(grp, j).start()

        own_out(grp).start()

    x_copy.wait()
    for grp in range(NG):
        forward_local(grp)

    @pl.loop(1, 8)
    def _(j):
        log_send(j).wait()

    def log_chip(at):
        at = lax.rem(at + 8, 4)
        return lbuf[at * 2] + lbuf[at * 2 + 1]

    def put(logs, i, v):
        return jnp.where(lane == i, v, logs)

    mine, other = lbuf[c], lbuf[y * 2 + 1 - k]
    logs = jnp.zeros((16, 128), F32)
    logs = put(logs, 0, jnp.where(core0, other, 0.0))
    logs = put(logs, 1, jnp.where(core0, 0.0, mine))
    logs = put(logs, 2, jnp.where(core0, 0.0, other))
    logs = put(logs, 4, log_chip(y - 1))
    logs = put(logs, 5, log_chip(y - 1) + log_chip(y - 2))
    logs = put(logs, 6, jnp.where(core0, 0.0, other))
    logs = put(logs, 7, jnp.where(core0, mine, 0.0))
    logs = put(logs, 8, jnp.where(core0, other, 0.0))
    logs = put(logs, 10, log_chip(y + 1))
    logs = put(logs, 11, log_chip(y + 1) + log_chip(y + 2))
    we[...] = mm(pack3(jnp.exp(logs))[:16], expand[...])
    own_g.wait()

    for grp in range(NG):
        forward_chip(grp)
    adjoint_local(0)
    adjoint_chip(0)
    forward_states(0)
    adjoint_local(1)
    adjoint_chip(1)
    forward_states(1)
    finish(0)
    adjoint_local(2)
    adjoint_chip(2)
    forward_states(2)
    finish(1)
    adjoint_local(3)
    adjoint_chip(3)
    forward_states(3)
    finish(2)
    finish(3)

    head_of = iota((COLS, 128), 0) // 64
    to_dc = jnp.where(iota((COLS, 128), 1) == head_of, 1.0, 0.0).astype(F32)
    tail = exact_mm(de[...], to_dc)
    tail = jnp.broadcast_to(tail[0:1, :], (128, 128)).T[0:16, 0:1]
    after = (iota((BLK, BLK), 0) >= iota((BLK, BLK), 1)).astype(F32)
    for blk in range(NBLK - 1, -1, -1):
        r = res[blk].T
        suffix = exact_mm(r[0:16], after) + tail
        tail = suffix[:, 0:1]
        at = slice(blk * BLK, (blk + 1) * BLK)
        sg_ref[:, at] = 16.0 * (r[64:80] / step_ref[:, at] - rate * suffix)

    for grp in range(NG):

        @pl.loop(1, NHEAD)
        def _(j):
            grad_in(grp, j).wait_send()
            grad_out(grp, j).wait()

        own_out(grp).wait()
        for dy in (1, 2, 3):

            @pl.when(y + dy < NY)
            def _():
                line_copy(fs_chip, fs_in, fys, fyr, grp, dy, True).wait_send()

            @pl.when(y - dy >= 0)
            def _():
                line_copy(as_chip, as_in, ays, ayr, grp, dy, False).wait_send()


def local(ssm_input, step_size, decay_rate, skip_gain, input_proj, output_proj, out_grad):
    vm = pltpu.VMEM
    dma = pltpu.SemaphoreType.DMA
    state = (NG, BLK, GC)
    proj = vm((LOCAL, BLK), BF16)
    scratch = [
        vm((LOCAL, COLS), BF16),
        vm((LOCAL, COLS), BF16),
        vm((LOCAL, COLS), BF16),
        vm((LOCAL, COLS), BF16),
        vm((2, LOCAL, GC), BF16),
        vm((2, LOCAL, GC), BF16),
        vm((NG, NBLK, BLK, GC), F32),
        vm((2, NBLK, BLK, GC), F32),
        vm((2, 2, CH * NGROUPS, BLK), BF16),
    ]
    scratch += [proj] * 8
    scratch += [
        vm((NBLK, BLK, 128), BF16),
        vm((NBLK, BLK, 128), BF16),
        vm((128, COLS), BF16),
        vm((BLK, GC), F32),
        vm((NBLK, BLK, 128), F32),
        vm((16, COLS), F32),
        vm((16, COLS), F32),
        vm((8, COLS), F32),
        vm((8, 16, 128), F32),
        vm(state, F32),
        vm(state, F32),
        vm(state, BF16),
        vm((3,) + state, BF16),
        vm(state, F32),
        vm(state, F32),
        vm(state, F32),
        vm((3,) + state, F32),
        dma((2 + NG,)),
        dma((2, 2)),
        dma((NG, NHEAD)), dma((NG, NHEAD)), dma((NG, NHEAD)), dma((NG, NHEAD)),
        dma((8,)), dma((8,)),
        dma((NG,)), dma((NG,)), dma((3, NG)), dma((3, NG)),
        dma((NG,)), dma((NG,)), dma((3, NG)), dma((3, NG)),
    ]
    hbm = pl.BlockSpec(memory_space=pl.ANY)
    vmem = pl.BlockSpec(memory_space=pltpu.VMEM)
    grads, steps = pl.pallas_call(
        kernel,
        out_shape=(
            jax.ShapeDtypeStruct((ROWS, NHEAD * COLS), BF16),
            jax.ShapeDtypeStruct((16, LOCAL), F32),
        ),
        in_specs=[hbm, vmem, vmem, vmem, hbm, hbm, hbm],
        out_specs=(hbm, vmem),
        scratch_shapes=scratch,
        compiler_params=pltpu.CompilerParams(
            collective_id=0, has_side_effects=True, vmem_limit_bytes=62 << 20
        ),
    )(
        ssm_input,
        step_size.T,
        decay_rate.reshape(1, 16),
        skip_gain.reshape(1, 16),
        input_proj.reshape(LOCAL * NGROUPS, BLK),
        output_proj.reshape(LOCAL * NGROUPS, BLK),
        out_grad,
    )
    return grads, steps.T


def solution(mesh):
    in_specs = (
        P("ctx", "head"),
        P("ctx", "head"),
        P("head"),
        P("head"),
        P("ctx", None, None),
        P("ctx", None, None),
        P(("ctx", "head"), None),
    )
    out_specs = (P(("ctx", "head"), None), P("ctx", "head"))
    return jax.shard_map(local, mesh=mesh, in_specs=in_specs, out_specs=out_specs, check_vma=False)
```

```python
import jax
import jax.numpy as jnp
from jax import lax
from jax.experimental import pallas as pl
from jax.experimental.pallas import tpu as pltpu
from jax.sharding import PartitionSpec as P

NHEAD = 16
NY = 4
LOCAL = 2048
ROWS = 128
COLS = 1024
BLK = 256
HALF = BLK // 2
NBLK = LOCAL // BLK
GC = 256
NG = COLS // GC
NGROUPS = 8
GAIN_ROW = 6 * NBLK
CH = 128
NCH = LOCAL // CH
MESH = pl.DeviceIdType.MESH
F32 = jnp.float32
BF16 = jnp.bfloat16


def mm(a, b):
    return jnp.dot(a, b, preferred_element_type=F32)


def exact_mm(a, b):
    return jnp.dot(a, b, preferred_element_type=F32, precision=lax.Precision.HIGHEST)


def twice(a):
    return jnp.concatenate([a, a], axis=1)


def whole(parts):
    return parts[:HALF].astype(F32) + parts[HALF:].astype(F32)


def halves(v):
    hi = v.astype(BF16)
    return hi, (v - hi.astype(F32)).astype(BF16)


def iota(shape, dim):
    return lax.broadcasted_iota(jnp.int32, shape, dim)


def pack3(v):
    hi = v.astype(BF16).astype(F32)
    rest = v - hi
    md = rest.astype(BF16).astype(F32)
    parts = jnp.concatenate([hi, md, rest - md, jnp.zeros((80, v.shape[1]), F32)], axis=0)
    return parts.T.astype(BF16)


def kernel(
    x_hbm, step_ref, rate_ref, gain_ref, b_hbm, c_hbm, g_hbm, out_hbm, sg_ref,
    xo, gv, xs, ags, tf, ta, raw, bm, cm, bt, ct, cbh, cbl, bch, bcl,
    asp, bsp, expand, acc, res, qe, we, de, lbuf,
    fs_tot, fs_pair, fs_chip, fs_in, as_tot, as_pair, as_chip, as_in,
    loc_sem, raw_sem, gs, gr, os, orr, ls, lr, fps, fpr, fys, fyr, aps, apr, ays, ayr,
):
    c = lax.axis_index("ctx")
    h = lax.axis_index("head")
    hx, hz = h // 4, lax.rem(h, 4)
    y, k = c // 2, lax.rem(c, 2)
    group = h // 2
    core0 = k == 0

    def head_at(j):
        return lax.rem(hx + j // 4, 4) * 4 + lax.rem(hz + lax.rem(j, 4), 4)

    def head_from(j):
        return lax.rem(hx + 4 - j // 4, 4) * 4 + lax.rem(hz + 4 - lax.rem(j, 4), 4)

    def cols(grp):
        return pl.ds(grp * GC, GC)

    x_copy = pltpu.make_async_copy(x_hbm, xo, loc_sem.at[0])
    x_copy.start()

    def raw_copies(i):
        rows = pl.ds(pl.multiple_of(i * (CH * NGROUPS), CH * NGROUPS), CH * NGROUPS)
        slot = lax.rem(i, 2)
        return (
            pltpu.make_async_copy(b_hbm.at[rows], raw.at[slot, 0], raw_sem.at[slot, 0]),
            pltpu.make_async_copy(c_hbm.at[rows], raw.at[slot, 1], raw_sem.at[slot, 1]),
        )

    for cp in raw_copies(0):
        cp.start()

    barrier = pltpu.get_barrier_semaphore()

    @pl.loop(1, NHEAD)
    def _(j):
        pl.semaphore_signal(barrier, 1, device_id=(c, head_at(j)), device_id_type=MESH)

    @pl.loop(1, 8)
    def _(j):
        pl.semaphore_signal(barrier, 1, device_id=(lax.rem(c + j, 8), h), device_id_type=MESH)

    pl.semaphore_wait(barrier, NHEAD - 1 + 7)

    def grad_in(grp, j):
        to = head_at(j)
        return pltpu.make_async_remote_copy(
            g_hbm.at[:, pl.ds(pl.multiple_of(to * COLS + grp * GC, GC), GC)],
            gv.at[pl.ds(pl.multiple_of(h * ROWS, ROWS), ROWS), cols(grp)],
            gs.at[grp, j],
            gr.at[grp, j],
            device_id=(c, to),
            device_id_type=MESH,
        )

    for grp in range(NG):

        @pl.loop(1, NHEAD)
        def _(j):
            grad_in(grp, j).start()

    own_g = pltpu.make_async_copy(
        g_hbm.at[:, pl.ds(pl.multiple_of(h * COLS, COLS), COLS)],
        gv.at[pl.ds(pl.multiple_of(h * ROWS, ROWS), ROWS)],
        loc_sem.at[1],
    )
    own_g.start()

    eye16 = iota((16, 16), 0) == iota((16, 16), 1)
    rate = jnp.sum(jnp.where(eye16, rate_ref[...], 0.0), axis=1, keepdims=True)
    gain = jnp.sum(jnp.where(eye16, gain_ref[...], 0.0), axis=1, keepdims=True)
    kk = iota((128, COLS), 0)
    expand[...] = jnp.where(
        (kk < 48) & (lax.rem(kk, 16) == iota((128, COLS), 1) // 64), 1.0, 0.0
    ).astype(BF16)
    before = (iota((BLK, BLK), 0) <= iota((BLK, BLK), 1)).astype(F32)
    lane = iota((16, 128), 1)
    logs = jnp.zeros((16, 128), F32)
    log_own = jnp.zeros((16, 1), F32)
    for blk in range(NBLK):
        st = step_ref[:, blk * BLK : (blk + 1) * BLK]
        cum = exact_mm(-rate * st, before)
        total = cum[:, BLK - 1 : BLK]
        half = cum[:, HALF - 1 : HALF]
        mid1, mid2 = 0.5 * half, 0.5 * (half + total)
        for row, v in enumerate((total, total - mid1, total - mid2, mid1, mid2, mid2 - mid1)):
            logs = jnp.where(lane == row * NBLK + blk, v, logs)
        log_own = log_own + total
        mid = jnp.where(iota((16, BLK), 1) < HALF, mid1, mid2)
        asp[blk] = pack3(jnp.exp(cum - mid))
        bsp[blk] = pack3(st * jnp.exp(mid - cum))
    qe[...] = mm(pack3(jnp.where(lane == GAIN_ROW, gain, jnp.exp(logs)))[:56], expand[...])
    lbuf[c] = jnp.broadcast_to(log_own, (16, 128))

    def log_send(j):
        return pltpu.make_async_remote_copy(
            lbuf.at[c], lbuf.at[c], ls.at[j], lr.at[j],
            device_id=(lax.rem(c + j, 8), h), device_id_type=MESH,
        )

    @pl.loop(1, 8)
    def _(j):
        log_send(j).start()

    pick = jnp.where(iota((32, 256), 1) == iota((32, 256), 0) * NGROUPS + group, 1.0, 0.0)
    pick = pick.astype(BF16)

    @pl.loop(0, NCH)
    def _(i):
        @pl.when(i + 1 < NCH)
        def _():
            for cp in raw_copies(i + 1):
                cp.start()

        for cp in raw_copies(i):
            cp.wait()
        slot = lax.rem(i, 2)
        at = pl.multiple_of(i * CH, CH)
        for which, target in ((0, bm), (1, cm)):
            for part in range(CH // 32):
                rows = raw[slot, which, pl.ds(part * 256, 256), :]
                target[pl.ds(at + part * 32, 32), :] = mm(pick, rows).astype(BF16)

    low = iota((BLK, BLK), 0) >= iota((BLK, BLK), 1)

    @pl.loop(0, NBLK)
    def _(blk):
        at = pl.ds(pl.multiple_of(blk * BLK, BLK), BLK)
        b, cc = bm[at, :], cm[at, :]
        btr, ctr = b.T, cc.T
        bt[at, :] = btr
        ct[at, :] = ctr
        cbh[at, :], cbl[at, :] = halves(jnp.where(low, mm(cc, btr), 0.0))
        bch[at, :], bcl[at, :] = halves(jnp.where(low, mm(cc, btr), 0.0).T)

    def pair_copy(src, dst, s, r, grp):
        return pltpu.make_async_remote_copy(
            src.at[grp], dst.at[grp], s.at[grp], r.at[grp],
            device_id=(y * 2 + 1 - k, h), device_id_type=MESH,
        )

    def line_copy(src, dst, s, r, grp, dy, forward):
        to = y + dy if forward else y + 4 - dy
        return pltpu.make_async_remote_copy(
            src.at[grp], dst.at[dy - 1, grp], s.at[dy - 1, grp], r.at[dy - 1, grp],
            device_id=(lax.rem(to, 4) * 2 + k, h), device_id_type=MESH,
        )

    def scale(which, blk, grp):
        return qe[pl.ds(which * NBLK + blk, 1), cols(grp)]

    def forward_local(grp):
        acc[...] = jnp.zeros_like(acc)

        @pl.loop(0, NBLK)
        def _(blk):
            at = pl.ds(pl.multiple_of(blk * BLK, BLK), BLK)
            t = jnp.zeros((BLK, GC), F32)
            for i in range(2):
                here = pl.ds(pl.multiple_of(blk * BLK + i * HALF, HALF), HALF)
                part = slice(i * HALF, (i + 1) * HALF)
                bs = mm(bsp[blk, part, :], expand[:, cols(grp)])
                pair = jnp.concatenate(halves(xo[here, cols(grp)].astype(F32) * bs), axis=0)
                xs[2 * blk + i, :, cols(grp)] = pair
                t = t + scale(1 + i, blk, grp) * mm(twice(bt[at, part]), pair)
            tf[grp, blk] = t
            acc[...] = scale(0, blk, grp) * acc[...] + t

        fs_tot[grp] = acc[...]
        pair_copy(fs_tot, fs_pair, fps, fpr, grp).start()

    def forward_chip(grp):
        pair_copy(fs_tot, fs_pair, fps, fpr, grp).wait()
        fs_chip[grp] = (
            we[0:1, cols(grp)] * fs_tot[grp] + we[1:2, cols(grp)] * fs_pair[grp]
        ).astype(BF16)
        for dy in (1, 2, 3):

            @pl.when(y + dy < NY)
            def _():
                line_copy(fs_chip, fs_in, fys, fyr, grp, dy, True).start()

    def forward_states(grp):
        acc[...] = jnp.zeros_like(acc)
        for dy in (1, 2, 3):

            @pl.when(y - dy >= 0)
            def _():
                line_copy(fs_chip, fs_in, fys, fyr, grp, dy, True).wait_recv()
                acc[...] += we[2 + dy : 3 + dy, cols(grp)] * fs_in[dy - 1, grp].astype(F32)

        acc[...] = we[2:3, cols(grp)] * acc[...]

        @pl.when(k == 1)
        def _():
            acc[...] += fs_pair[grp]

        @pl.loop(0, NBLK)
        def _(blk):
            entry = acc[...]
            acc[...] = scale(0, blk, grp) * entry + tf[grp, blk]
            tf[grp, blk] = entry

        tf[grp, NBLK] = acc[...]

    def adjoint_local(grp):
        slot = grp % 2

        @pl.loop(1, NHEAD)
        def _(j):
            grad_in(grp, j).wait_recv()

        acc[...] = jnp.zeros_like(acc)

        @pl.loop(0, NBLK)
        def _(lap):
            blk = NBLK - 1 - lap
            at = pl.ds(pl.multiple_of(blk * BLK, BLK), BLK)
            t = jnp.zeros((BLK, GC), F32)
            for i in range(2):
                here = pl.ds(pl.multiple_of(blk * BLK + i * HALF, HALF), HALF)
                part = slice(i * HALF, (i + 1) * HALF)
                a = mm(asp[blk, part, :], expand[:, cols(grp)])
                pair = jnp.concatenate(halves(gv[here, cols(grp)].astype(F32) * a), axis=0)
                ags[slot, 2 * blk + i] = pair
                t = t + scale(3 + i, blk, grp) * mm(twice(ct[at, part]), pair)
            ta[slot, blk] = t
            acc[...] = scale(0, blk, grp) * acc[...] + t

        as_tot[grp] = acc[...]
        pair_copy(as_tot, as_pair, aps, apr, grp).start()

    def adjoint_chip(grp):
        pair_copy(as_tot, as_pair, aps, apr, grp).wait()
        as_chip[grp] = we[6:7, cols(grp)] * as_tot[grp] + we[7:8, cols(grp)] * as_pair[grp]
        for dy in (1, 2, 3):

            @pl.when(y - dy >= 0)
            def _():
                line_copy(as_chip, as_in, ays, ayr, grp, dy, False).start()

    def grad_out(grp, j):
        to = head_at(j)
        return pltpu.make_async_remote_copy(
            xo.at[pl.ds(pl.multiple_of(to * ROWS, ROWS), ROWS), cols(grp)],
            out_hbm.at[:, pl.ds(pl.multiple_of(h * COLS + grp * GC, GC), GC)],
            os.at[grp, j],
            orr.at[grp, j],
            device_id=(c, to),
            device_id_type=MESH,
        )

    def own_out(grp):
        return pltpu.make_async_copy(
            xo.at[pl.ds(pl.multiple_of(h * ROWS, ROWS), ROWS), cols(grp)],
            out_hbm.at[:, pl.ds(pl.multiple_of(h * COLS + grp * GC, GC), GC)],
            loc_sem.at[2 + grp],
        )

    def finish(grp):
        slot = grp % 2
        acc[...] = jnp.zeros_like(acc)
        for dy in (1, 2, 3):

            @pl.when(y + dy < NY)
            def _():
                line_copy(as_chip, as_in, ays, ayr, grp, dy, False).wait_recv()
                acc[...] += we[8 + dy : 9 + dy, cols(grp)] * as_in[dy - 1, grp]

        acc[...] = we[8:9, cols(grp)] * acc[...]

        @pl.when(core0)
        def _():
            acc[...] += as_pair[grp]

        gain_row = qe[GAIN_ROW : GAIN_ROW + 1, cols(grp)]
        head_of = grp * (GC // 64) + iota((GC, 128), 0) // 64
        to_dc = jnp.where(iota((GC, 128), 1) == head_of, 1.0, 0.0).astype(BF16)
        to_sx = jnp.where(iota((GC, 128), 1) == head_of + 64, 1.0, 0.0).astype(BF16)

        @pl.loop(0, NBLK)
        def _(lap):
            blk = NBLK - 1 - lap
            at = pl.ds(pl.multiple_of(blk * BLK, BLK), BLK)
            first, second = slice(0, HALF), slice(HALF, BLK)
            entry = acc[...]
            acc[...] = scale(0, blk, grp) * entry + ta[slot, blk]
            tails = jnp.sum(tf[grp, blk + 1] * entry, axis=0, keepdims=True)
            de[pl.ds(blk, 1), cols(grp)] = tails
            sh, sl = halves(entry)
            b, ph, plo = bm[at, :], bch[at, :], bcl[at, :]
            inter = mm(b, sh) + mm(b, sl)
            a1, a2 = ags[slot, 2 * blk], ags[slot, 2 * blk + 1]
            p2 = mm(twice(ph[:, second]), a2) + mm(plo[:, second], a2[:HALF])
            p1 = mm(twice(ph[first, first]), a1) + mm(plo[first, first], a1[:HALF])
            cross = scale(5, blk, grp)
            gbs = (
                p1 + cross * p2[first] + scale(1, blk, grp) * inter[first],
                p2[second] + scale(2, blk, grp) * inter[second],
            )
            sh, sl = halves(tf[grp, blk])
            cc, ph, plo = cm[at, :], cbh[at, :], cbl[at, :]
            inter = mm(cc, sh) + mm(cc, sl)
            x1, x2 = xs[2 * blk, :, cols(grp)], xs[2 * blk + 1, :, cols(grp)]
            p1 = mm(twice(ph[:, first]), x1) + mm(plo[:, first], x1[:HALF])
            p2 = mm(twice(ph[second, second]), x2) + mm(plo[second, second], x2[:HALF])
            ys = (
                p1[first] + scale(3, blk, grp) * inter[first],
                p2 + cross * p1[second] + scale(4, blk, grp) * inter[second],
            )
            for i, (xx, aa) in enumerate(((x1, a1), (x2, a2))):
                here = pl.ds(pl.multiple_of(blk * BLK + i * HALF, HALF), HALF)
                part = slice(i * HALF, (i + 1) * HALF)
                bs = mm(bsp[blk, part, :], expand[:, cols(grp)])
                grads = bs * gbs[i] + gain_row * gv[here, cols(grp)].astype(F32)
                xo[here, cols(grp)] = grads.astype(BF16)
                sx = whole(xx) * gbs[i]
                dc = whole(aa) * ys[i] - sx
                dh, dl = halves(dc)
                gh, gl = halves(sx)
                r = mm(dh, to_dc) + mm(dl, to_dc) + mm(gh, to_sx) + mm(gl, to_sx)
                if grp == 0:
                    res[blk, part, :] = r
                else:
                    res[blk, part, :] += r

        @pl.loop(1, NHEAD)
        def _(j):
            grad_out(grp, j).start()

        own_out(grp).start()

    x_copy.wait()
    for grp in range(NG):
        forward_local(grp)

    @pl.loop(1, 8)
    def _(j):
        log_send(j).wait()

    def log_chip(at):
        at = lax.rem(at + 8, 4)
        return lbuf[at * 2] + lbuf[at * 2 + 1]

    def put(logs, i, v):
        return jnp.where(lane == i, v, logs)

    mine, other = lbuf[c], lbuf[y * 2 + 1 - k]
    logs = jnp.zeros((16, 128), F32)
    logs = put(logs, 0, jnp.where(core0, other, 0.0))
    logs = put(logs, 1, jnp.where(core0, 0.0, mine))
    logs = put(logs, 2, jnp.where(core0, 0.0, other))
    logs = put(logs, 4, log_chip(y - 1))
    logs = put(logs, 5, log_chip(y - 1) + log_chip(y - 2))
    logs = put(logs, 6, jnp.where(core0, 0.0, other))
    logs = put(logs, 7, jnp.where(core0, mine, 0.0))
    logs = put(logs, 8, jnp.where(core0, other, 0.0))
    logs = put(logs, 10, log_chip(y + 1))
    logs = put(logs, 11, log_chip(y + 1) + log_chip(y + 2))
    we[...] = mm(pack3(jnp.exp(logs))[:16], expand[...])
    own_g.wait()

    for grp in range(NG):
        forward_chip(grp)
    adjoint_local(0)
    adjoint_chip(0)
    forward_states(0)
    adjoint_local(1)
    adjoint_chip(1)
    forward_states(1)
    finish(0)
    adjoint_local(2)
    adjoint_chip(2)
    forward_states(2)
    finish(1)
    adjoint_local(3)
    adjoint_chip(3)
    forward_states(3)
    finish(2)
    finish(3)

    head_of = iota((COLS, 128), 0) // 64
    to_dc = jnp.where(iota((COLS, 128), 1) == head_of, 1.0, 0.0).astype(F32)
    tails = jnp.concatenate([exact_mm(de[...], to_dc), jnp.zeros((120, 128), F32)], axis=0).T
    after = (iota((BLK, BLK), 0) >= iota((BLK, BLK), 1)).astype(F32)
    for blk in range(NBLK):
        r = res[blk].T
        suffix = exact_mm(r[0:16], after) + tails[0:16, blk : blk + 1]
        at = slice(blk * BLK, (blk + 1) * BLK)
        sg_ref[:, at] = r[64:80] / step_ref[:, at] - rate * suffix

    for grp in range(NG):

        @pl.loop(1, NHEAD)
        def _(j):
            grad_in(grp, j).wait_send()
            grad_out(grp, j).wait()

        own_out(grp).wait()
        for dy in (1, 2, 3):

            @pl.when(y + dy < NY)
            def _():
                line_copy(fs_chip, fs_in, fys, fyr, grp, dy, True).wait_send()

            @pl.when(y - dy >= 0)
            def _():
                line_copy(as_chip, as_in, ays, ayr, grp, dy, False).wait_send()


def local(ssm_input, step_size, decay_rate, skip_gain, input_proj, output_proj, out_grad):
    vm = pltpu.VMEM
    dma = pltpu.SemaphoreType.DMA
    state = (NG, BLK, GC)
    proj = vm((LOCAL, BLK), BF16)
    scratch = [
        vm((LOCAL, COLS), BF16),
        vm((LOCAL, COLS), BF16),
        vm((2 * NBLK, BLK, COLS), BF16),
        vm((2, 2 * NBLK, BLK, GC), BF16),
        vm((NG, NBLK + 1, BLK, GC), F32),
        vm((2, NBLK, BLK, GC), F32),
        vm((2, 2, CH * NGROUPS, BLK), BF16),
    ]
    scratch += [proj] * 8
    scratch += [
        vm((NBLK, BLK, 128), BF16),
        vm((NBLK, BLK, 128), BF16),
        vm((128, COLS), BF16),
        vm((BLK, GC), F32),
        vm((NBLK, BLK, 128), F32),
        vm((56, COLS), F32),
        vm((16, COLS), F32),
        vm((8, COLS), F32),
        vm((8, 16, 128), F32),
        vm(state, F32),
        vm(state, F32),
        vm(state, BF16),
        vm((3,) + state, BF16),
        vm(state, F32),
        vm(state, F32),
        vm(state, F32),
        vm((3,) + state, F32),
        dma((2 + NG,)),
        dma((2, 2)),
        dma((NG, NHEAD)), dma((NG, NHEAD)), dma((NG, NHEAD)), dma((NG, NHEAD)),
        dma((8,)), dma((8,)),
        dma((NG,)), dma((NG,)), dma((3, NG)), dma((3, NG)),
        dma((NG,)), dma((NG,)), dma((3, NG)), dma((3, NG)),
    ]
    hbm = pl.BlockSpec(memory_space=pl.ANY)
    vmem = pl.BlockSpec(memory_space=pltpu.VMEM)
    grads, steps = pl.pallas_call(
        kernel,
        out_shape=(
            jax.ShapeDtypeStruct((ROWS, NHEAD * COLS), BF16),
            jax.ShapeDtypeStruct((16, LOCAL), F32),
        ),
        in_specs=[hbm, vmem, vmem, vmem, hbm, hbm, hbm],
        out_specs=(hbm, vmem),
        scratch_shapes=scratch,
        compiler_params=pltpu.CompilerParams(
            collective_id=0, has_side_effects=True, vmem_limit_bytes=62 << 20
        ),
    )(
        ssm_input,
        step_size.T,
        decay_rate.reshape(1, 16),
        skip_gain.reshape(1, 16),
        input_proj.reshape(LOCAL * NGROUPS, BLK),
        output_proj.reshape(LOCAL * NGROUPS, BLK),
        out_grad,
    )
    return grads, steps.T


def solution(mesh):
    in_specs = (
        P("ctx", "head"),
        P("ctx", "head"),
        P("head"),
        P("head"),
        P("ctx", None, None),
        P("ctx", None, None),
        P(("ctx", "head"), None),
    )
    out_specs = (P(("ctx", "head"), None), P("ctx", "head"))
    return jax.shard_map(local, mesh=mesh, in_specs=in_specs, out_specs=out_specs, check_vma=False)
```

```python
import jax
import jax.numpy as jnp
from jax import lax
from jax.experimental import pallas as pl
from jax.experimental.pallas import tpu as pltpu
from jax.sharding import PartitionSpec as P

NHEAD = 16
NY = 4
LOCAL = 2048
ROWS = 128
COLS = 1024
BLK = 256
HALF = BLK // 2
NBLK = LOCAL // BLK
GC = 256
NG = COLS // GC
NGROUPS = 8
GAIN_ROW = 6 * NBLK
CH = 128
NCH = LOCAL // CH
MESH = pl.DeviceIdType.MESH
F32 = jnp.float32
BF16 = jnp.bfloat16


def mm(a, b):
    return jnp.dot(a, b, preferred_element_type=F32)


def exact_mm(a, b):
    return jnp.dot(a, b, preferred_element_type=F32, precision=lax.Precision.HIGHEST)


def twice(a):
    return jnp.concatenate([a, a], axis=1)


def whole(parts):
    return parts[:HALF].astype(F32) + parts[HALF:].astype(F32)


def halves(v):
    hi = v.astype(BF16)
    return hi, (v - hi.astype(F32)).astype(BF16)


def iota(shape, dim):
    return lax.broadcasted_iota(jnp.int32, shape, dim)


def pack3(v):
    hi = v.astype(BF16).astype(F32)
    rest = v - hi
    md = rest.astype(BF16).astype(F32)
    parts = jnp.concatenate([hi, md, rest - md, jnp.zeros((80, v.shape[1]), F32)], axis=0)
    return parts.T.astype(BF16)


def kernel(
    x_hbm, step_ref, rate_ref, gain_ref, b_hbm, c_hbm, g_hbm, out_hbm, sg_ref,
    xo, gv, xs, ags, tf, ta, raw, wide, bm, cm, bt, ct, cbh, cbl, bch, bcl,
    asp, bsp, expand, acc, res, qe, we, de, lbuf,
    fs_tot, fs_pair, fs_chip, fs_in, fs_half, as_tot, as_pair, as_chip, as_in, as_half,
    loc_sem, raw_sem, gs, gr, os, orr, ls, lr, fps, fpr, fys, fyr, fhs, fhr, aps, apr, ays, ayr, ahs, ahr,
):
    c = lax.axis_index("ctx")
    h = lax.axis_index("head")
    hx, hz = h // 4, lax.rem(h, 4)
    y, k = c // 2, lax.rem(c, 2)
    group = h // 2
    core0 = k == 0

    def head_at(j):
        return lax.rem(hx + j // 4, 4) * 4 + lax.rem(hz + lax.rem(j, 4), 4)

    def head_from(j):
        return lax.rem(hx + 4 - j // 4, 4) * 4 + lax.rem(hz + 4 - lax.rem(j, 4), 4)

    def cols(grp):
        return pl.ds(grp * GC, GC)

    x_copy = pltpu.make_async_copy(x_hbm, xo, loc_sem.at[0])
    x_copy.start()

    def raw_copies(i):
        rows = pl.ds(pl.multiple_of(i * (CH * NGROUPS), CH * NGROUPS), CH * NGROUPS)
        slot = lax.rem(i, 2)
        return (
            pltpu.make_async_copy(b_hbm.at[rows], raw.at[slot, 0], raw_sem.at[slot, 0]),
            pltpu.make_async_copy(c_hbm.at[rows], raw.at[slot, 1], raw_sem.at[slot, 1]),
        )

    for cp in raw_copies(0):
        cp.start()

    barrier = pltpu.get_barrier_semaphore()

    @pl.loop(1, NHEAD)
    def _(j):
        pl.semaphore_signal(barrier, 1, device_id=(c, head_at(j)), device_id_type=MESH)

    @pl.loop(1, 8)
    def _(j):
        pl.semaphore_signal(barrier, 1, device_id=(lax.rem(c + j, 8), h), device_id_type=MESH)

    pl.semaphore_wait(barrier, NHEAD - 1 + 7)

    def grad_in(grp, j):
        to = head_at(j)
        return pltpu.make_async_remote_copy(
            g_hbm.at[:, pl.ds(pl.multiple_of(to * COLS + grp * GC, GC), GC)],
            gv.at[pl.ds(pl.multiple_of(h * ROWS, ROWS), ROWS), cols(grp)],
            gs.at[grp, j],
            gr.at[grp, j],
            device_id=(c, to),
            device_id_type=MESH,
        )

    def send_grad(grp):
        @pl.loop(1, NHEAD)
        def _(j):
            grad_in(grp, j).start()

    send_grad(0)
    send_grad(1)
    own_g = pltpu.make_async_copy(
        g_hbm.at[:, pl.ds(pl.multiple_of(h * COLS, COLS), COLS)],
        gv.at[pl.ds(pl.multiple_of(h * ROWS, ROWS), ROWS)],
        loc_sem.at[1],
    )
    own_g.start()

    eye16 = iota((16, 16), 0) == iota((16, 16), 1)
    rate = jnp.sum(jnp.where(eye16, rate_ref[...], 0.0), axis=1, keepdims=True)
    gain = jnp.sum(jnp.where(eye16, gain_ref[...], 0.0), axis=1, keepdims=True)
    kk = iota((128, COLS), 0)
    expand[...] = jnp.where(
        (kk < 48) & (lax.rem(kk, 16) == iota((128, COLS), 1) // 64), 1.0, 0.0
    ).astype(BF16)
    before = (iota((BLK, BLK), 0) <= iota((BLK, BLK), 1)).astype(F32)
    lane = iota((16, 128), 1)
    logs = jnp.zeros((16, 128), F32)
    log_own = jnp.zeros((16, 1), F32)
    for blk in range(NBLK):
        st = step_ref[:, blk * BLK : (blk + 1) * BLK]
        cum = exact_mm(-rate * st, before)
        total = cum[:, BLK - 1 : BLK]
        half = cum[:, HALF - 1 : HALF]
        mid1, mid2 = 0.5 * half, 0.5 * (half + total)
        for row, v in enumerate((total, total - mid1, total - mid2, mid1, mid2, mid2 - mid1)):
            logs = jnp.where(lane == row * NBLK + blk, v, logs)
        log_own = log_own + total
        mid = jnp.where(iota((16, BLK), 1) < HALF, mid1, mid2)
        asp[blk] = pack3(jnp.exp(cum - mid))
        bsp[blk] = pack3(st * jnp.exp(mid - cum))
    qe[...] = mm(pack3(jnp.where(lane == GAIN_ROW, gain, jnp.exp(logs)))[:56], expand[...])
    lbuf[c] = jnp.broadcast_to(log_own, (16, 128))

    def log_send(j):
        return pltpu.make_async_remote_copy(
            lbuf.at[c], lbuf.at[c], ls.at[j], lr.at[j],
            device_id=(lax.rem(c + j, 8), h), device_id_type=MESH,
        )

    @pl.loop(1, 8)
    def _(j):
        log_send(j).start()

    @pl.loop(0, NCH)
    def _(i):
        @pl.when(i + 1 < NCH)
        def _():
            for cp in raw_copies(i + 1):
                cp.start()

        for cp in raw_copies(i):
            cp.wait()
        slot = lax.rem(i, 2)
        at = pl.multiple_of(i * CH, CH)
        for which, target in ((0, bm), (1, cm)):
            for n in range(2):
                lanes = slice(n * 128, n * 128 + 128)
                wide[which, n] = raw[slot, which, :, lanes].astype(F32)
                rows = wide[which, n, pl.ds(group, CH, stride=NGROUPS), :]
                target[pl.ds(at, CH), lanes] = rows.astype(BF16)

    low = iota((BLK, BLK), 0) >= iota((BLK, BLK), 1)

    @pl.loop(0, NBLK)
    def _(blk):
        at = pl.ds(pl.multiple_of(blk * BLK, BLK), BLK)
        b, cc = bm[at, :], cm[at, :]
        btr, ctr = b.T, cc.T
        bt[at, :] = btr
        ct[at, :] = ctr
        cbh[at, :], cbl[at, :] = halves(jnp.where(low, mm(cc, btr), 0.0))
        bch[at, :], bcl[at, :] = halves(jnp.where(low, mm(cc, btr), 0.0).T)

    def pair_copy(src, dst, s, r, grp):
        return pltpu.make_async_remote_copy(
            src.at[grp], dst.at[grp], s.at[grp], r.at[grp],
            device_id=(y * 2 + 1 - k, h), device_id_type=MESH,
        )

    def line_copy(src, dst, s, r, grp, dy, forward):
        to = y + dy if forward else y + 4 - dy
        return pltpu.make_async_remote_copy(
            src.at[grp], dst.at[dy - 1, grp], s.at[dy - 1, grp], r.at[dy - 1, grp],
            device_id=(lax.rem(to, 4) * 2 + k, h), device_id_type=MESH,
        )

    def half_copy(ref, s, r, grp):
        return pltpu.make_async_remote_copy(
            ref.at[grp, k], ref.at[grp, k], s.at[grp], r.at[grp],
            device_id=(y * 2 + 1 - k, h), device_id_type=MESH,
        )

    my_half = pl.ds(pl.multiple_of(k * HALF, HALF), HALF)

    def scale(which, blk, grp):
        return qe[pl.ds(which * NBLK + blk, 1), cols(grp)]

    def forward_local(grp):
        acc[...] = jnp.zeros_like(acc)

        @pl.loop(0, NBLK)
        def _(blk):
            at = pl.ds(pl.multiple_of(blk * BLK, BLK), BLK)
            t = jnp.zeros((BLK, GC), F32)
            for i in range(2):
                here = pl.ds(pl.multiple_of(blk * BLK + i * HALF, HALF), HALF)
                part = slice(i * HALF, (i + 1) * HALF)
                bs = mm(bsp[blk, part, :], expand[:, cols(grp)])
                pair = jnp.concatenate(halves(xo[here, cols(grp)].astype(F32) * bs), axis=0)
                xs[2 * blk + i, :, cols(grp)] = pair
                t = t + scale(1 + i, blk, grp) * mm(twice(bt[at, part]), pair)
            tf[grp, blk] = t
            acc[...] = scale(0, blk, grp) * acc[...] + t

        fs_tot[grp] = acc[...]
        pair_copy(fs_tot, fs_pair, fps, fpr, grp).start()

    def forward_chip(grp):
        pair_copy(fs_tot, fs_pair, fps, fpr, grp).wait()
        fs_chip[grp] = (
            we[0:1, cols(grp)] * fs_tot[grp, my_half, :]
            + we[1:2, cols(grp)] * fs_pair[grp, my_half, :]
        ).astype(BF16)
        for dy in (1, 2, 3):

            @pl.when(y + dy < NY)
            def _():
                line_copy(fs_chip, fs_in, fys, fyr, grp, dy, True).start()

    def forward_half(grp):
        fs_half[grp, k] = jnp.zeros((HALF, GC), F32)
        for dy in (1, 2, 3):

            @pl.when(y - dy >= 0)
            def _():
                line_copy(fs_chip, fs_in, fys, fyr, grp, dy, True).wait_recv()
                fs_half[grp, k] += we[2 + dy : 3 + dy, cols(grp)] * fs_in[dy - 1, grp].astype(F32)

        half_copy(fs_half, fhs, fhr, grp).start()

    def forward_states(grp):
        half_copy(fs_half, fhs, fhr, grp).wait()
        acc[0:HALF, :] = we[2:3, cols(grp)] * fs_half[grp, 0]
        acc[HALF:BLK, :] = we[2:3, cols(grp)] * fs_half[grp, 1]

        @pl.when(k == 1)
        def _():
            acc[...] += fs_pair[grp]

        @pl.loop(0, NBLK)
        def _(blk):
            entry = acc[...]
            acc[...] = scale(0, blk, grp) * entry + tf[grp, blk]
            tf[grp, blk] = entry

        tf[grp, NBLK] = acc[...]

    def adjoint_local(grp):
        slot = grp % 2

        @pl.loop(1, NHEAD)
        def _(j):
            grad_in(grp, j).wait_recv()

        acc[...] = jnp.zeros_like(acc)

        @pl.loop(0, NBLK)
        def _(lap):
            blk = NBLK - 1 - lap
            at = pl.ds(pl.multiple_of(blk * BLK, BLK), BLK)
            t = jnp.zeros((BLK, GC), F32)
            for i in range(2):
                here = pl.ds(pl.multiple_of(blk * BLK + i * HALF, HALF), HALF)
                part = slice(i * HALF, (i + 1) * HALF)
                a = mm(asp[blk, part, :], expand[:, cols(grp)])
                pair = jnp.concatenate(halves(gv[here, cols(grp)].astype(F32) * a), axis=0)
                ags[slot, 2 * blk + i] = pair
                t = t + scale(3 + i, blk, grp) * mm(twice(ct[at, part]), pair)
            ta[slot, blk] = t
            acc[...] = scale(0, blk, grp) * acc[...] + t

        as_tot[grp] = acc[...]
        pair_copy(as_tot, as_pair, aps, apr, grp).start()

    def adjoint_chip(grp):
        pair_copy(as_tot, as_pair, aps, apr, grp).wait()
        as_chip[grp] = (
            we[6:7, cols(grp)] * as_tot[grp, my_half, :]
            + we[7:8, cols(grp)] * as_pair[grp, my_half, :]
        )
        for dy in (1, 2, 3):

            @pl.when(y - dy >= 0)
            def _():
                line_copy(as_chip, as_in, ays, ayr, grp, dy, False).start()

    def adjoint_half(grp):
        as_half[grp, k] = jnp.zeros((HALF, GC), F32)
        for dy in (1, 2, 3):

            @pl.when(y + dy < NY)
            def _():
                line_copy(as_chip, as_in, ays, ayr, grp, dy, False).wait_recv()
                as_half[grp, k] += we[8 + dy : 9 + dy, cols(grp)] * as_in[dy - 1, grp]

        half_copy(as_half, ahs, ahr, grp).start()

    def grad_out(grp, j):
        to = head_at(j)
        return pltpu.make_async_remote_copy(
            xo.at[pl.ds(pl.multiple_of(to * ROWS, ROWS), ROWS), cols(grp)],
            out_hbm.at[:, pl.ds(pl.multiple_of(h * COLS + grp * GC, GC), GC)],
            os.at[grp, j],
            orr.at[grp, j],
            device_id=(c, to),
            device_id_type=MESH,
        )

    def own_out(grp):
        return pltpu.make_async_copy(
            xo.at[pl.ds(pl.multiple_of(h * ROWS, ROWS), ROWS), cols(grp)],
            out_hbm.at[:, pl.ds(pl.multiple_of(h * COLS + grp * GC, GC), GC)],
            loc_sem.at[2 + grp],
        )

    def finish(grp):
        slot = grp % 2
        half_copy(as_half, ahs, ahr, grp).wait()
        acc[0:HALF, :] = we[8:9, cols(grp)] * as_half[grp, 0]
        acc[HALF:BLK, :] = we[8:9, cols(grp)] * as_half[grp, 1]

        @pl.when(core0)
        def _():
            acc[...] += as_pair[grp]

        gain_row = qe[GAIN_ROW : GAIN_ROW + 1, cols(grp)]
        head_of = grp * (GC // 64) + iota((GC, 128), 0) // 64
        to_dc = jnp.where(iota((GC, 128), 1) == head_of, 1.0, 0.0).astype(BF16)
        to_sx = jnp.where(iota((GC, 128), 1) == head_of + 64, 1.0, 0.0).astype(BF16)

        @pl.loop(0, NBLK)
        def _(lap):
            blk = NBLK - 1 - lap
            at = pl.ds(pl.multiple_of(blk * BLK, BLK), BLK)
            first, second = slice(0, HALF), slice(HALF, BLK)
            entry = acc[...]
            acc[...] = scale(0, blk, grp) * entry + ta[slot, blk]
            tails = jnp.sum(tf[grp, blk + 1] * entry, axis=0, keepdims=True)
            de[pl.ds(blk, 1), cols(grp)] = tails
            sh, sl = halves(entry)
            b, ph, plo = bm[at, :], bch[at, :], bcl[at, :]
            inter = mm(b, sh) + mm(b, sl)
            a1, a2 = ags[slot, 2 * blk], ags[slot, 2 * blk + 1]
            p2 = mm(twice(ph[:, second]), a2) + mm(plo[:, second], a2[:HALF])
            p1 = mm(twice(ph[first, first]), a1) + mm(plo[first, first], a1[:HALF])
            cross = scale(5, blk, grp)
            gbs = (
                p1 + cross * p2[first] + scale(1, blk, grp) * inter[first],
                p2[second] + scale(2, blk, grp) * inter[second],
            )
            sh, sl = halves(tf[grp, blk])
            cc, ph, plo = cm[at, :], cbh[at, :], cbl[at, :]
            inter = mm(cc, sh) + mm(cc, sl)
            x1, x2 = xs[2 * blk, :, cols(grp)], xs[2 * blk + 1, :, cols(grp)]
            p1 = mm(twice(ph[:, first]), x1) + mm(plo[:, first], x1[:HALF])
            p2 = mm(twice(ph[second, second]), x2) + mm(plo[second, second], x2[:HALF])
            ys = (
                p1[first] + scale(3, blk, grp) * inter[first],
                p2 + cross * p1[second] + scale(4, blk, grp) * inter[second],
            )
            for i, (xx, aa) in enumerate(((x1, a1), (x2, a2))):
                here = pl.ds(pl.multiple_of(blk * BLK + i * HALF, HALF), HALF)
                part = slice(i * HALF, (i + 1) * HALF)
                bs = mm(bsp[blk, part, :], expand[:, cols(grp)])
                grads = bs * gbs[i] + gain_row * gv[here, cols(grp)].astype(F32)
                xo[here, cols(grp)] = grads.astype(BF16)
                sx = whole(xx) * gbs[i]
                dc = whole(aa) * ys[i] - sx
                dh, dl = halves(dc)
                gh, gl = halves(sx)
                r = mm(dh, to_dc) + mm(dl, to_dc) + mm(gh, to_sx) + mm(gl, to_sx)
                if grp == 0:
                    res[blk, part, :] = r
                else:
                    res[blk, part, :] += r

        @pl.loop(1, NHEAD)
        def _(j):
            grad_out(grp, j).start()

        own_out(grp).start()

    @pl.loop(1, 8)
    def _(j):
        log_send(j).wait()

    def log_chip(at):
        at = lax.rem(at + 8, 4)
        return lbuf[at * 2] + lbuf[at * 2 + 1]

    def put(logs, i, v):
        return jnp.where(lane == i, v, logs)

    mine, other = lbuf[c], lbuf[y * 2 + 1 - k]
    logs = jnp.zeros((16, 128), F32)
    logs = put(logs, 0, jnp.where(core0, other, 0.0))
    logs = put(logs, 1, jnp.where(core0, 0.0, mine))
    logs = put(logs, 2, jnp.where(core0, 0.0, other))
    logs = put(logs, 4, log_chip(y - 1))
    logs = put(logs, 5, log_chip(y - 1) + log_chip(y - 2))
    logs = put(logs, 6, jnp.where(core0, 0.0, other))
    logs = put(logs, 7, jnp.where(core0, mine, 0.0))
    logs = put(logs, 8, jnp.where(core0, other, 0.0))
    logs = put(logs, 10, log_chip(y + 1))
    logs = put(logs, 11, log_chip(y + 1) + log_chip(y + 2))
    we[...] = mm(pack3(jnp.exp(logs))[:16], expand[...])
    x_copy.wait()
    own_g.wait()

    send_grad(2)
    adjoint_local(0)
    send_grad(3)
    forward_local(0)
    adjoint_chip(0)
    forward_chip(0)
    forward_local(1)
    adjoint_half(0)
    forward_half(0)
    forward_chip(1)
    adjoint_local(1)
    forward_states(0)
    finish(0)
    for grp in range(1, NG):
        adjoint_chip(grp)
        if grp + 1 < NG:
            forward_local(grp + 1)
        forward_half(grp)
        if grp + 1 < NG:
            forward_chip(grp + 1)
        adjoint_half(grp)
        if grp + 1 < NG:
            adjoint_local(grp + 1)
        forward_states(grp)
        finish(grp)

    head_of = iota((COLS, 128), 0) // 64
    to_dc = jnp.where(iota((COLS, 128), 1) == head_of, 1.0, 0.0).astype(F32)
    tails = jnp.concatenate([exact_mm(de[...], to_dc), jnp.zeros((120, 128), F32)], axis=0).T
    after = (iota((BLK, BLK), 0) >= iota((BLK, BLK), 1)).astype(F32)
    for blk in range(NBLK):
        r = res[blk].T
        suffix = exact_mm(r[0:16], after) + tails[0:16, blk : blk + 1]
        at = slice(blk * BLK, (blk + 1) * BLK)
        sg_ref[:, at] = r[64:80] / step_ref[:, at] - rate * suffix

    for grp in range(NG):

        @pl.loop(1, NHEAD)
        def _(j):
            grad_in(grp, j).wait_send()
            grad_out(grp, j).wait()

        own_out(grp).wait()
        for dy in (1, 2, 3):

            @pl.when(y + dy < NY)
            def _():
                line_copy(fs_chip, fs_in, fys, fyr, grp, dy, True).wait_send()

            @pl.when(y - dy >= 0)
            def _():
                line_copy(as_chip, as_in, ays, ayr, grp, dy, False).wait_send()


def local(ssm_input, step_size, decay_rate, skip_gain, input_proj, output_proj, out_grad):
    vm = pltpu.VMEM
    dma = pltpu.SemaphoreType.DMA
    state = (NG, BLK, GC)
    half = (NG, HALF, GC)
    proj = vm((LOCAL, BLK), BF16)
    scratch = [
        vm((LOCAL, COLS), BF16),
        vm((LOCAL, COLS), BF16),
        vm((2 * NBLK, BLK, COLS), BF16),
        vm((2, 2 * NBLK, BLK, GC), BF16),
        vm((NG, NBLK + 1, BLK, GC), F32),
        vm((2, NBLK, BLK, GC), F32),
        vm((2, 2, CH * NGROUPS, BLK), BF16),
    ]
    scratch += [vm((2, 2, CH * NGROUPS, 128), F32)]
    scratch += [proj] * 8
    scratch += [
        vm((NBLK, BLK, 128), BF16),
        vm((NBLK, BLK, 128), BF16),
        vm((128, COLS), BF16),
        vm((BLK, GC), F32),
        vm((NBLK, BLK, 128), F32),
        vm((56, COLS), F32),
        vm((16, COLS), F32),
        vm((8, COLS), F32),
        vm((8, 16, 128), F32),
        vm(state, F32),
        vm(state, F32),
        vm(half, BF16),
        vm((3,) + half, BF16),
        vm((NG, 2, HALF, GC), F32),
        vm(state, F32),
        vm(state, F32),
        vm(half, F32),
        vm((3,) + half, F32),
        vm((NG, 2, HALF, GC), F32),
        dma((2 + NG,)),
        dma((2, 2)),
        dma((NG, NHEAD)), dma((NG, NHEAD)), dma((NG, NHEAD)), dma((NG, NHEAD)),
        dma((8,)), dma((8,)),
        dma((NG,)), dma((NG,)), dma((3, NG)), dma((3, NG)), dma((NG,)), dma((NG,)),
        dma((NG,)), dma((NG,)), dma((3, NG)), dma((3, NG)), dma((NG,)), dma((NG,)),
    ]
    hbm = pl.BlockSpec(memory_space=pl.ANY)
    vmem = pl.BlockSpec(memory_space=pltpu.VMEM)
    grads, steps = pl.pallas_call(
        kernel,
        out_shape=(
            jax.ShapeDtypeStruct((ROWS, NHEAD * COLS), BF16),
            jax.ShapeDtypeStruct((16, LOCAL), F32),
        ),
        in_specs=[hbm, vmem, vmem, vmem, hbm, hbm, hbm],
        out_specs=(hbm, vmem),
        scratch_shapes=scratch,
        compiler_params=pltpu.CompilerParams(
            collective_id=0, has_side_effects=True, vmem_limit_bytes=62 << 20
        ),
    )(
        ssm_input,
        step_size.T,
        decay_rate.reshape(1, 16),
        skip_gain.reshape(1, 16),
        input_proj.reshape(LOCAL * NGROUPS, BLK),
        output_proj.reshape(LOCAL * NGROUPS, BLK),
        out_grad,
    )
    return grads, steps.T


def solution(mesh):
    in_specs = (
        P("ctx", "head"),
        P("ctx", "head"),
        P("head"),
        P("head"),
        P("ctx", None, None),
        P("ctx", None, None),
        P(("ctx", "head"), None),
    )
    out_specs = (P(("ctx", "head"), None), P("ctx", "head"))
    return jax.shard_map(local, mesh=mesh, in_specs=in_specs, out_specs=out_specs, check_vma=False)
```

```python
import jax
import jax.numpy as jnp
from jax import lax
from jax.experimental import pallas as pl
from jax.experimental.pallas import tpu as pltpu
from jax.sharding import PartitionSpec as P

NHEAD = 16
NY = 4
LOCAL = 2048
ROWS = 128
COLS = 1024
BLK = 256
HALF = BLK // 2
NBLK = LOCAL // BLK
GC = 256
NG = COLS // GC
NGROUPS = 8
GAIN_ROW = 6 * NBLK
CH = 128
NCH = LOCAL // CH
MESH = pl.DeviceIdType.MESH
ORDER = (10, 5, 15, 7, 13, 6, 14, 9, 11, 2, 8, 1, 3, 4, 12)
F32 = jnp.float32
BF16 = jnp.bfloat16


def mm(a, b):
    return jnp.dot(a, b, preferred_element_type=F32)


def exact_mm(a, b):
    return jnp.dot(a, b, preferred_element_type=F32, precision=lax.Precision.HIGHEST)


def twice(a):
    return jnp.concatenate([a, a], axis=1)


def whole(parts):
    return parts[:HALF].astype(F32) + parts[HALF:].astype(F32)


def halves(v):
    hi = v.astype(BF16)
    return hi, (v - hi.astype(F32)).astype(BF16)


def iota(shape, dim):
    return lax.broadcasted_iota(jnp.int32, shape, dim)


def pack3(v):
    hi = v.astype(BF16).astype(F32)
    rest = v - hi
    md = rest.astype(BF16).astype(F32)
    parts = jnp.concatenate([hi, md, rest - md, jnp.zeros((80, v.shape[1]), F32)], axis=0)
    return parts.T.astype(BF16)


def kernel(
    x_hbm, step_ref, rate_ref, gain_ref, b_hbm, c_hbm, g_hbm, out_hbm, sg_ref,
    xo, gv, xs, ags, tf, ta, raw, wide, bm, cm, bt, ct, cbh, cbl, bch, bcl,
    asp, bsp, expand, acc, res, qe, we, de, lbuf,
    fs_tot, fs_pair, fs_chip, fs_in, fs_half, as_tot, as_pair, as_chip, as_in, as_half,
    loc_sem, raw_sem, gs, gr, os, orr, ls, lr, fps, fpr, fys, fyr, fhs, fhr, aps, apr, ays, ayr, ahs, ahr,
):
    c = lax.axis_index("ctx")
    h = lax.axis_index("head")
    hx, hz = h // 4, lax.rem(h, 4)
    y, k = c // 2, lax.rem(c, 2)
    group = h // 2
    core0 = k == 0

    def head_at(j):
        return lax.rem(hx + j // 4, 4) * 4 + lax.rem(hz + (j - (j // 4) * 4), 4)

    def head_from(j):
        return lax.rem(hx + 4 - j // 4, 4) * 4 + lax.rem(hz + 4 - (j - (j // 4) * 4), 4)

    def cols(grp):
        return pl.ds(grp * GC, GC)

    x_copy = pltpu.make_async_copy(x_hbm, xo, loc_sem.at[0])
    x_copy.start()

    def raw_copies(i):
        rows = pl.ds(pl.multiple_of(i * (CH * NGROUPS), CH * NGROUPS), CH * NGROUPS)
        slot = lax.rem(i, 2)
        return (
            pltpu.make_async_copy(b_hbm.at[rows], raw.at[slot, 0], raw_sem.at[slot, 0]),
            pltpu.make_async_copy(c_hbm.at[rows], raw.at[slot, 1], raw_sem.at[slot, 1]),
        )

    for cp in raw_copies(0):
        cp.start()

    barrier = pltpu.get_barrier_semaphore()

    @pl.loop(1, NHEAD)
    def _(j):
        pl.semaphore_signal(barrier, 1, device_id=(c, head_at(j)), device_id_type=MESH)

    @pl.loop(1, 8)
    def _(j):
        pl.semaphore_signal(barrier, 1, device_id=(lax.rem(c + j, 8), h), device_id_type=MESH)

    pl.semaphore_wait(barrier, NHEAD - 1 + 7)

    def grad_in(grp, j):
        to = head_at(j)
        return pltpu.make_async_remote_copy(
            g_hbm.at[:, pl.ds(pl.multiple_of(to * COLS + grp * GC, GC), GC)],
            gv.at[pl.ds(pl.multiple_of(h * ROWS, ROWS), ROWS), cols(grp)],
            gs.at[grp, j],
            gr.at[grp, j],
            device_id=(c, to),
            device_id_type=MESH,
        )

    def send_grad(grp):
        for j in ORDER:
            grad_in(grp, j).start()

    send_grad(0)
    send_grad(1)
    own_g = pltpu.make_async_copy(
        g_hbm.at[:, pl.ds(pl.multiple_of(h * COLS, COLS), COLS)],
        gv.at[pl.ds(pl.multiple_of(h * ROWS, ROWS), ROWS)],
        loc_sem.at[1],
    )
    own_g.start()

    eye16 = iota((16, 16), 0) == iota((16, 16), 1)
    rate = jnp.sum(jnp.where(eye16, rate_ref[...], 0.0), axis=1, keepdims=True)
    gain = jnp.sum(jnp.where(eye16, gain_ref[...], 0.0), axis=1, keepdims=True)
    kk = iota((128, COLS), 0)
    expand[...] = jnp.where(
        (kk < 48) & (lax.rem(kk, 16) == iota((128, COLS), 1) // 64), 1.0, 0.0
    ).astype(BF16)
    before = (iota((BLK, BLK), 0) <= iota((BLK, BLK), 1)).astype(F32)
    lane = iota((16, 128), 1)
    logs = jnp.zeros((16, 128), F32)
    log_own = jnp.zeros((16, 1), F32)
    for blk in range(NBLK):
        st = step_ref[:, blk * BLK : (blk + 1) * BLK]
        cum = exact_mm(-rate * st, before)
        total = cum[:, BLK - 1 : BLK]
        half = cum[:, HALF - 1 : HALF]
        mid1, mid2 = 0.5 * half, 0.5 * (half + total)
        for row, v in enumerate((total, total - mid1, total - mid2, mid1, mid2, mid2 - mid1)):
            logs = jnp.where(lane == row * NBLK + blk, v, logs)
        log_own = log_own + total
        mid = jnp.where(iota((16, BLK), 1) < HALF, mid1, mid2)
        asp[blk] = pack3(jnp.exp(cum - mid))
        bsp[blk] = pack3(st * jnp.exp(mid - cum))
    qe[...] = mm(pack3(jnp.where(lane == GAIN_ROW, gain, jnp.exp(logs)))[:56], expand[...])
    lbuf[c] = jnp.broadcast_to(log_own, (16, 128))

    def log_send(j):
        return pltpu.make_async_remote_copy(
            lbuf.at[c], lbuf.at[c], ls.at[j], lr.at[j],
            device_id=(lax.rem(c + j, 8), h), device_id_type=MESH,
        )

    @pl.loop(1, 8)
    def _(j):
        log_send(j).start()

    @pl.loop(0, NCH)
    def _(i):
        @pl.when(i + 1 < NCH)
        def _():
            for cp in raw_copies(i + 1):
                cp.start()

        for cp in raw_copies(i):
            cp.wait()
        slot = lax.rem(i, 2)
        at = pl.multiple_of(i * CH, CH)
        for which, target in ((0, bm), (1, cm)):
            for n in range(2):
                lanes = slice(n * 128, n * 128 + 128)
                wide[which, n] = raw[slot, which, :, lanes].astype(F32)
                rows = wide[which, n, pl.ds(group, CH, stride=NGROUPS), :]
                target[pl.ds(at, CH), lanes] = rows.astype(BF16)

    low = iota((BLK, BLK), 0) >= iota((BLK, BLK), 1)

    @pl.loop(0, NBLK)
    def _(blk):
        at = pl.ds(pl.multiple_of(blk * BLK, BLK), BLK)
        b, cc = bm[at, :], cm[at, :]
        btr, ctr = b.T, cc.T
        bt[at, :] = btr
        ct[at, :] = ctr
        cbh[at, :], cbl[at, :] = halves(jnp.where(low, mm(cc, btr), 0.0))
        bch[at, :], bcl[at, :] = halves(jnp.where(low, mm(cc, btr), 0.0).T)

    def pair_copy(src, dst, s, r, grp):
        return pltpu.make_async_remote_copy(
            src.at[grp], dst.at[grp], s.at[grp], r.at[grp],
            device_id=(y * 2 + 1 - k, h), device_id_type=MESH,
        )

    def line_copy(src, dst, s, r, grp, dy, forward):
        to = y + dy if forward else y + 4 - dy
        return pltpu.make_async_remote_copy(
            src.at[grp], dst.at[dy - 1, grp], s.at[dy - 1, grp], r.at[dy - 1, grp],
            device_id=(lax.rem(to, 4) * 2 + k, h), device_id_type=MESH,
        )

    def half_copy(ref, s, r, grp):
        return pltpu.make_async_remote_copy(
            ref.at[grp, k], ref.at[grp, k], s.at[grp], r.at[grp],
            device_id=(y * 2 + 1 - k, h), device_id_type=MESH,
        )

    my_half = pl.ds(pl.multiple_of(k * HALF, HALF), HALF)

    def scale(which, blk, grp):
        return qe[pl.ds(which * NBLK + blk, 1), cols(grp)]

    def forward_local(grp):
        acc[...] = jnp.zeros_like(acc)

        @pl.loop(0, NBLK)
        def _(blk):
            at = pl.ds(pl.multiple_of(blk * BLK, BLK), BLK)
            t = jnp.zeros((BLK, GC), F32)
            for i in range(2):
                here = pl.ds(pl.multiple_of(blk * BLK + i * HALF, HALF), HALF)
                part = slice(i * HALF, (i + 1) * HALF)
                bs = mm(bsp[blk, part, :], expand[:, cols(grp)])
                pair = jnp.concatenate(halves(xo[here, cols(grp)].astype(F32) * bs), axis=0)
                xs[2 * blk + i, :, cols(grp)] = pair
                t = t + scale(1 + i, blk, grp) * mm(twice(bt[at, part]), pair)
            tf[grp, blk] = t
            acc[...] = scale(0, blk, grp) * acc[...] + t

        fs_tot[grp] = acc[...]
        pair_copy(fs_tot, fs_pair, fps, fpr, grp).start()

    def forward_chip(grp):
        pair_copy(fs_tot, fs_pair, fps, fpr, grp).wait()
        fs_chip[grp] = (
            we[0:1, cols(grp)] * fs_tot[grp, my_half, :]
            + we[1:2, cols(grp)] * fs_pair[grp, my_half, :]
        ).astype(BF16)
        for dy in (1, 2, 3):

            @pl.when(y + dy < NY)
            def _():
                line_copy(fs_chip, fs_in, fys, fyr, grp, dy, True).start()

    def forward_half(grp):
        fs_half[grp, k] = jnp.zeros((HALF, GC), F32)
        for dy in (1, 2, 3):

            @pl.when(y - dy >= 0)
            def _():
                line_copy(fs_chip, fs_in, fys, fyr, grp, dy, True).wait_recv()
                fs_half[grp, k] += we[2 + dy : 3 + dy, cols(grp)] * fs_in[dy - 1, grp].astype(F32)

        half_copy(fs_half, fhs, fhr, grp).start()

    def forward_states(grp):
        half_copy(fs_half, fhs, fhr, grp).wait()
        acc[0:HALF, :] = we[2:3, cols(grp)] * fs_half[grp, 0]
        acc[HALF:BLK, :] = we[2:3, cols(grp)] * fs_half[grp, 1]

        @pl.when(k == 1)
        def _():
            acc[...] += fs_pair[grp]

        @pl.loop(0, NBLK)
        def _(blk):
            entry = acc[...]
            acc[...] = scale(0, blk, grp) * entry + tf[grp, blk]
            tf[grp, blk] = entry

        tf[grp, NBLK] = acc[...]

    def adjoint_local(grp):
        slot = grp % 2

        @pl.loop(1, NHEAD)
        def _(j):
            grad_in(grp, j).wait_recv()

        acc[...] = jnp.zeros_like(acc)

        @pl.loop(0, NBLK)
        def _(lap):
            blk = NBLK - 1 - lap
            at = pl.ds(pl.multiple_of(blk * BLK, BLK), BLK)
            t = jnp.zeros((BLK, GC), F32)
            for i in range(2):
                here = pl.ds(pl.multiple_of(blk * BLK + i * HALF, HALF), HALF)
                part = slice(i * HALF, (i + 1) * HALF)
                a = mm(asp[blk, part, :], expand[:, cols(grp)])
                pair = jnp.concatenate(halves(gv[here, cols(grp)].astype(F32) * a), axis=0)
                ags[slot, 2 * blk + i] = pair
                t = t + scale(3 + i, blk, grp) * mm(twice(ct[at, part]), pair)
            ta[slot, blk] = t
            acc[...] = scale(0, blk, grp) * acc[...] + t

        as_tot[grp] = acc[...]
        pair_copy(as_tot, as_pair, aps, apr, grp).start()

    def adjoint_chip(grp):
        pair_copy(as_tot, as_pair, aps, apr, grp).wait()
        as_chip[grp] = (
            we[6:7, cols(grp)] * as_tot[grp, my_half, :]
            + we[7:8, cols(grp)] * as_pair[grp, my_half, :]
        )
        for dy in (1, 2, 3):

            @pl.when(y - dy >= 0)
            def _():
                line_copy(as_chip, as_in, ays, ayr, grp, dy, False).start()

    def adjoint_half(grp):
        as_half[grp, k] = jnp.zeros((HALF, GC), F32)
        for dy in (1, 2, 3):

            @pl.when(y + dy < NY)
            def _():
                line_copy(as_chip, as_in, ays, ayr, grp, dy, False).wait_recv()
                as_half[grp, k] += we[8 + dy : 9 + dy, cols(grp)] * as_in[dy - 1, grp]

        half_copy(as_half, ahs, ahr, grp).start()

    def grad_out(grp, j):
        to = head_at(j)
        return pltpu.make_async_remote_copy(
            xo.at[pl.ds(pl.multiple_of(to * ROWS, ROWS), ROWS), cols(grp)],
            out_hbm.at[:, pl.ds(pl.multiple_of(h * COLS + grp * GC, GC), GC)],
            os.at[grp, j],
            orr.at[grp, j],
            device_id=(c, to),
            device_id_type=MESH,
        )

    def own_out(grp):
        return pltpu.make_async_copy(
            xo.at[pl.ds(pl.multiple_of(h * ROWS, ROWS), ROWS), cols(grp)],
            out_hbm.at[:, pl.ds(pl.multiple_of(h * COLS + grp * GC, GC), GC)],
            loc_sem.at[2 + grp],
        )

    def finish(grp):
        slot = grp % 2
        half_copy(as_half, ahs, ahr, grp).wait()
        acc[0:HALF, :] = we[8:9, cols(grp)] * as_half[grp, 0]
        acc[HALF:BLK, :] = we[8:9, cols(grp)] * as_half[grp, 1]

        @pl.when(core0)
        def _():
            acc[...] += as_pair[grp]

        gain_row = qe[GAIN_ROW : GAIN_ROW + 1, cols(grp)]
        head_of = grp * (GC // 64) + iota((GC, 128), 0) // 64
        to_dc = jnp.where(iota((GC, 128), 1) == head_of, 1.0, 0.0).astype(BF16)
        to_sx = jnp.where(iota((GC, 128), 1) == head_of + 64, 1.0, 0.0).astype(BF16)

        @pl.loop(0, NBLK)
        def _(lap):
            blk = NBLK - 1 - lap
            at = pl.ds(pl.multiple_of(blk * BLK, BLK), BLK)
            first, second = slice(0, HALF), slice(HALF, BLK)
            entry = acc[...]
            acc[...] = scale(0, blk, grp) * entry + ta[slot, blk]
            tails = jnp.sum(tf[grp, blk + 1] * entry, axis=0, keepdims=True)
            de[pl.ds(blk, 1), cols(grp)] = tails
            sh, sl = halves(entry)
            b, ph, plo = bm[at, :], bch[at, :], bcl[at, :]
            inter = mm(b, sh) + mm(b, sl)
            a1, a2 = ags[slot, 2 * blk], ags[slot, 2 * blk + 1]
            p2 = mm(twice(ph[:, second]), a2) + mm(plo[:, second], a2[:HALF])
            p1 = mm(twice(ph[first, first]), a1) + mm(plo[first, first], a1[:HALF])
            cross = scale(5, blk, grp)
            gbs = (
                p1 + cross * p2[first] + scale(1, blk, grp) * inter[first],
                p2[second] + scale(2, blk, grp) * inter[second],
            )
            cc, ph, plo = cm[at, :], cbh[at, :], cbl[at, :]
            inter = mm(cc, tf[grp, blk].astype(BF16))
            x1, x2 = xs[2 * blk, :, cols(grp)], xs[2 * blk + 1, :, cols(grp)]
            p1 = mm(twice(ph[:, first]), x1) + mm(plo[:, first], x1[:HALF])
            p2 = mm(twice(ph[second, second]), x2) + mm(plo[second, second], x2[:HALF])
            ys = (
                p1[first] + scale(3, blk, grp) * inter[first],
                p2 + cross * p1[second] + scale(4, blk, grp) * inter[second],
            )
            for i, (xx, aa) in enumerate(((x1, a1), (x2, a2))):
                here = pl.ds(pl.multiple_of(blk * BLK + i * HALF, HALF), HALF)
                part = slice(i * HALF, (i + 1) * HALF)
                bs = mm(bsp[blk, part, :], expand[:, cols(grp)])
                grads = bs * gbs[i] + gain_row * gv[here, cols(grp)].astype(F32)
                xo[here, cols(grp)] = grads.astype(BF16)
                sx = whole(xx) * gbs[i]
                dc = whole(aa) * ys[i] - sx
                dh, dl = halves(dc)
                gh, gl = halves(sx)
                r = mm(dh, to_dc) + mm(dl, to_dc) + mm(gh, to_sx) + mm(gl, to_sx)
                if grp == 0:
                    res[blk, part, :] = r
                else:
                    res[blk, part, :] += r

        for j in ORDER:
            grad_out(grp, j).start()

        own_out(grp).start()

    @pl.loop(1, 8)
    def _(j):
        log_send(j).wait()

    def log_chip(at):
        at = lax.rem(at + 8, 4)
        return lbuf[at * 2] + lbuf[at * 2 + 1]

    def put(logs, i, v):
        return jnp.where(lane == i, v, logs)

    mine, other = lbuf[c], lbuf[y * 2 + 1 - k]
    logs = jnp.zeros((16, 128), F32)
    logs = put(logs, 0, jnp.where(core0, other, 0.0))
    logs = put(logs, 1, jnp.where(core0, 0.0, mine))
    logs = put(logs, 2, jnp.where(core0, 0.0, other))
    logs = put(logs, 4, log_chip(y - 1))
    logs = put(logs, 5, log_chip(y - 1) + log_chip(y - 2))
    logs = put(logs, 6, jnp.where(core0, 0.0, other))
    logs = put(logs, 7, jnp.where(core0, mine, 0.0))
    logs = put(logs, 8, jnp.where(core0, other, 0.0))
    logs = put(logs, 10, log_chip(y + 1))
    logs = put(logs, 11, log_chip(y + 1) + log_chip(y + 2))
    we[...] = mm(pack3(jnp.exp(logs))[:16], expand[...])
    x_copy.wait()
    own_g.wait()

    send_grad(2)
    adjoint_local(0)
    send_grad(3)
    forward_local(0)
    adjoint_chip(0)
    forward_chip(0)
    forward_local(1)
    adjoint_half(0)
    forward_half(0)
    forward_chip(1)
    adjoint_local(1)
    forward_states(0)
    finish(0)
    for grp in range(1, NG):
        adjoint_chip(grp)
        if grp + 1 < NG:
            forward_local(grp + 1)
        forward_half(grp)
        if grp + 1 < NG:
            forward_chip(grp + 1)
        adjoint_half(grp)
        if grp + 1 < NG:
            adjoint_local(grp + 1)
        forward_states(grp)
        finish(grp)

    head_of = iota((COLS, 128), 0) // 64
    to_dc = jnp.where(iota((COLS, 128), 1) == head_of, 1.0, 0.0).astype(F32)
    tails = jnp.concatenate([exact_mm(de[...], to_dc), jnp.zeros((120, 128), F32)], axis=0).T
    after = (iota((BLK, BLK), 0) >= iota((BLK, BLK), 1)).astype(F32)
    for blk in range(NBLK):
        r = res[blk].T
        suffix = exact_mm(r[0:16], after) + tails[0:16, blk : blk + 1]
        at = slice(blk * BLK, (blk + 1) * BLK)
        sg_ref[:, at] = r[64:80] / step_ref[:, at] - rate * suffix

    for grp in range(NG):

        @pl.loop(1, NHEAD)
        def _(j):
            grad_in(grp, j).wait_send()
            grad_out(grp, j).wait()

        own_out(grp).wait()
        for dy in (1, 2, 3):

            @pl.when(y + dy < NY)
            def _():
                line_copy(fs_chip, fs_in, fys, fyr, grp, dy, True).wait_send()

            @pl.when(y - dy >= 0)
            def _():
                line_copy(as_chip, as_in, ays, ayr, grp, dy, False).wait_send()


def local(ssm_input, step_size, decay_rate, skip_gain, input_proj, output_proj, out_grad):
    vm = pltpu.VMEM
    dma = pltpu.SemaphoreType.DMA
    state = (NG, BLK, GC)
    half = (NG, HALF, GC)
    proj = vm((LOCAL, BLK), BF16)
    scratch = [
        vm((LOCAL, COLS), BF16),
        vm((LOCAL, COLS), BF16),
        vm((2 * NBLK, BLK, COLS), BF16),
        vm((2, 2 * NBLK, BLK, GC), BF16),
        vm((NG, NBLK + 1, BLK, GC), F32),
        vm((2, NBLK, BLK, GC), F32),
        vm((2, 2, CH * NGROUPS, BLK), BF16),
    ]
    scratch += [vm((2, 2, CH * NGROUPS, 128), F32)]
    scratch += [proj] * 8
    scratch += [
        vm((NBLK, BLK, 128), BF16),
        vm((NBLK, BLK, 128), BF16),
        vm((128, COLS), BF16),
        vm((BLK, GC), F32),
        vm((NBLK, BLK, 128), F32),
        vm((56, COLS), F32),
        vm((16, COLS), F32),
        vm((8, COLS), F32),
        vm((8, 16, 128), F32),
        vm(state, F32),
        vm(state, F32),
        vm(half, BF16),
        vm((3,) + half, BF16),
        vm((NG, 2, HALF, GC), F32),
        vm(state, F32),
        vm(state, F32),
        vm(half, F32),
        vm((3,) + half, F32),
        vm((NG, 2, HALF, GC), F32),
        dma((2 + NG,)),
        dma((2, 2)),
        dma((NG, NHEAD)), dma((NG, NHEAD)), dma((NG, NHEAD)), dma((NG, NHEAD)),
        dma((8,)), dma((8,)),
        dma((NG,)), dma((NG,)), dma((3, NG)), dma((3, NG)), dma((NG,)), dma((NG,)),
        dma((NG,)), dma((NG,)), dma((3, NG)), dma((3, NG)), dma((NG,)), dma((NG,)),
    ]
    hbm = pl.BlockSpec(memory_space=pl.ANY)
    vmem = pl.BlockSpec(memory_space=pltpu.VMEM)
    grads, steps = pl.pallas_call(
        kernel,
        out_shape=(
            jax.ShapeDtypeStruct((ROWS, NHEAD * COLS), BF16),
            jax.ShapeDtypeStruct((16, LOCAL), F32),
        ),
        in_specs=[hbm, vmem, vmem, vmem, hbm, hbm, hbm],
        out_specs=(hbm, vmem),
        scratch_shapes=scratch,
        compiler_params=pltpu.CompilerParams(
            collective_id=0, has_side_effects=True, vmem_limit_bytes=62 << 20
        ),
    )(
        ssm_input,
        step_size.T,
        decay_rate.reshape(1, 16),
        skip_gain.reshape(1, 16),
        input_proj.reshape(LOCAL * NGROUPS, BLK),
        output_proj.reshape(LOCAL * NGROUPS, BLK),
        out_grad,
    )
    return grads, steps.T


def solution(mesh):
    in_specs = (
        P("ctx", "head"),
        P("ctx", "head"),
        P("head"),
        P("head"),
        P("ctx", None, None),
        P("ctx", None, None),
        P(("ctx", "head"), None),
    )
    out_specs = (P(("ctx", "head"), None), P("ctx", "head"))
    return jax.shard_map(local, mesh=mesh, in_specs=in_specs, out_specs=out_specs, check_vma=False)
```
